32 devices in a mesh: groups: 2 (over x), expert: 4 (over z), tensor: 4 (over y, core).
Axes of the slice: x: 2, y: 2, z: 4, core: 2. Of those that a mesh axis runs over, the one named last changes fastest.
Arguments:
- context: bfloat16 [512, 3072], P(('groups', 'expert'), 'tensor'), parts along dimension 0, may hold values from -6 to 6
- out_proj: bfloat16 [3072, 3072], P('tensor'), may hold values from -0.109375 to 0.109375
- resid: bfloat16 [512, 3072], P(('groups', 'expert')), parts along dimension 0, may hold values from -6 to 6
- norm_gain: bfloat16 [3072], replicated, may hold values from 0.099609375 to 1.8984375
- routes: int32 [512, 2], P(('groups', 'expert')), parts along dimension 0, may hold values from 0 to 3, all different within a row; in each aligned block of 16 rows (0 to 15, 16 to 31, ...) at most 8 rows name the same one
- gates: float32 [512, 2], P(('groups', 'expert', 'tensor')), parts along dimension 0, may hold values from 0.1 to 1
- w_gate: bfloat16 [4, 3072, 8192], P('expert', None, 'tensor'), may hold values from -0.109375 to 0.109375
- w_up: bfloat16 [4, 3072, 8192], P('expert', None, 'tensor'), may hold values from -0.109375 to 0.109375
- w_down: bfloat16 [4, 8192, 3072], P('expert', 'tensor'), may hold values from -0.0625 to 0.0625
Outputs:
- mixed: bfloat16 [512, 3072], P(('groups', 'expert', 'tensor')), parts along dimension 0
The draws below stay inside these ranges and needn't reach their ends.
There are 2 independent parts, one for each index of `groups`. The reference program is written for one: setup_inputs(seed, part) draws one part's arguments, and reference() takes and returns one part's arrays. A program takes and returns all parts, laid end to end along the dimension named above; an argument that names none is the same for every part. Nothing has to cross between parts.
Inputs may be any that keep to these rules, and one draw needn't show every extreme that they name: `routes`: the two experts of a row differ; in each aligned block of 16 rows (the rows of one device) no expert is named by more than 8 rows.
All inputs are finite; a program needn't handle non-finite values.
Results may differ from the reference program's by a relative error of at most 0.0041.
Values may be sent and summed in bfloat16 or wider, within the bound.
A program may use at most 128 MiB of HBM per device.

```python
import math
import jax
import jax.numpy as jnp
import numpy as np
from jax import lax

D = 3072
HD = 3072
FF = 8192
TOK_DEV = 16
EXPERTS = 4
CAP_DEV = 8
TOKENS = 256


def shard_levels(stream_key, shape, shards, low, top_value):
    loudness, own = 1.0, jax.random.fold_in(stream_key, 6)
    for position, blocks in shards:
        heights = jnp.exp(jax.random.uniform(jax.random.fold_in(own, position), (blocks,), jnp.float32, low / len(shards), top_value / len(shards)))
        loudness = loudness * jnp.repeat(heights, shape[position] // blocks).reshape([-1 if axis == position else 1 for axis in range(len(shape))])
    return loudness


def shared_out(rng, own, number, rows, number_of, top, limit, skew):
    ranking = jax.random.permutation(rng, number_of)
    heavy_load, common = portions_of(number_of, rows * top, limit, skew, True), portions_of(number_of, rows * top, limit, skew, False)
    places = jnp.arange(number_of)

    def named(sizes, rotation):
        used = int((sizes > 0).sum())
        fixed = max(1, used // 4)
        moved = fixed + (places - fixed + rotation * (used - fixed)) % max(1, number_of - fixed)
        return jnp.zeros((number_of,), jnp.int32).at[ranking[jnp.where(places < fixed, places, moved)]].set(jnp.asarray(sizes, jnp.int32))

    sizes = jnp.where(number % 4 == 0, named(heavy_load, number // 4), named(common, number - number // 4 - 1))
    mixed = jax.random.permutation(jax.random.fold_in(own, 3), number_of)
    source_of, sink = mixed[0:number_of // 2 * 2:2], mixed[1:number_of // 2 * 2:2]
    margin = jnp.minimum(sizes[source_of] - 1, limit - sizes[sink]) // 2
    margin = jnp.where((source_of == ranking[0]) | (sink == ranking[0]) | (sizes[sink] == 0), 0, jnp.maximum(margin, 0))
    moved = jax.random.randint(jax.random.fold_in(own, 4), (number_of // 2,), 0, 1 << 20) % (margin + 1)
    sizes = sizes.at[source_of].add(-moved).at[sink].add(moved)
    labels = jnp.searchsorted(jnp.cumsum(sizes), jnp.arange(rows * top), side="right").astype(jnp.int32)
    table = labels.reshape(top, rows).T
    table = table[jax.random.permutation(jax.random.fold_in(own, 1), rows)]
    rotation = jax.random.randint(jax.random.fold_in(own, 2), (rows, 1), 0, top)
    return jnp.take_along_axis(table, (jnp.arange(top)[None, :] + rotation) % top, axis=1)


def portions_of(amount, total, limit, skew, full):
    portions = [(1 << 20) // math.isqrt(grade ** skew) + 1 for grade in range(1, amount + 1)]
    largest = limit if full else min(limit, max(-(-total // amount), total * portions[0] // sum(portions)))
    least = 1 if total - largest >= amount - 1 else 0
    counts, spare = [largest] + [least] * (amount - 1), total - largest - least * (amount - 1)
    while spare > 0:
        movable = [i for i in range(1, amount) if counts[i] < largest] or [i for i in range(1, amount) if counts[i] < limit]
        whole, left = sum([portions[i] for i in movable]), spare
        for i in movable:
            addition = min(limit - counts[i], max(1, left * portions[i] // whole), spare)
            counts[i] = counts[i] + addition
            spare = spare - addition
    return np.array(counts)


def gaussian(own_key, extent, deviation, bound, pieces=(), held_as=jnp.bfloat16):
    drawn = deviation * jax.random.normal(own_key, extent, jnp.float32)
    if pieces:
        drawn = drawn * shard_levels(own_key, extent, pieces, -0.22, 0.18)
    return jnp.clip(drawn, -bound, bound).astype(held_as)


def setup_inputs(seed: int = 0, part: int = 0) -> dict:
    arg_keys = jax.random.split(jax.random.key(seed), 10)
    own_keys = jax.random.split(jax.random.fold_in(arg_keys[9], part), 10)
    context = gaussian(own_keys[0], (TOKENS, HD), 1.0, 6.0, ((0, 4), (1, 4)))
    out_proj = gaussian(arg_keys[1], (HD, D), HD ** -0.5, 0.109375, ((0, 4),))
    resid = gaussian(own_keys[2], (TOKENS, D), 1.0, 6.0, ((0, 4),))
    norm_gain = jnp.clip(1.0 + 0.18 * jax.random.normal(arg_keys[3], (D,), jnp.float32), 0.099609375, 1.8984375).astype(jnp.bfloat16)
    routes_keys = jax.random.split(jax.random.fold_in(own_keys[4], 1), TOKENS // TOK_DEV)
    routes_turns = jax.random.permutation(jax.random.fold_in(own_keys[4], 3), TOKENS // TOK_DEV)
    routes = jax.vmap(lambda own, number: shared_out(jax.random.fold_in(own_keys[4], 2), own, number, TOK_DEV, EXPERTS, 2, CAP_DEV, 2))(routes_keys, routes_turns).reshape((TOKENS, 2))
    gates = jnp.clip(0.1 + 0.9 * jax.random.uniform(own_keys[5], (TOKENS, 2), jnp.float32) ** shard_levels(own_keys[5], (TOKENS, 2), ((0, 16),), -0.2, 0.2), 0.1, 1.0)
    w_gate = gaussian(arg_keys[6], (EXPERTS, D, FF), D ** -0.5, 0.109375, ((0, 4), (2, 4)))
    w_up = gaussian(arg_keys[7], (EXPERTS, D, FF), D ** -0.5, 0.109375, ((0, 4), (2, 4)))
    w_down = gaussian(arg_keys[8], (EXPERTS, FF, D), FF ** -0.5, 0.0625, ((0, 4), (1, 4)))
    return {"context": context, "out_proj": out_proj, "resid": resid, "norm_gain": norm_gain, "routes": routes, "gates": gates, "w_gate": w_gate, "w_up": w_up, "w_down": w_down}


def expert_apply(args):
    rows, gate_w, up_w, down_w = args
    gate = jnp.dot(rows, gate_w, preferred_element_type=jnp.float32)
    upper = jnp.dot(rows, up_w, preferred_element_type=jnp.float32)
    hidden = (jax.nn.silu(gate) * upper).astype(jnp.bfloat16)
    return jnp.dot(hidden, down_w, preferred_element_type=jnp.float32).astype(jnp.bfloat16)

def reference(context, out_proj, resid, norm_gain, routes, gates, w_gate, w_up, w_down):
    state = resid.astype(jnp.float32) + jnp.dot(context, out_proj, preferred_element_type=jnp.float32)
    scale = lax.rsqrt(lax.optimization_barrier(jnp.mean(state * state, axis=-1, keepdims=True)) + 1e-05)
    normed = (state * scale * norm_gain.astype(jnp.float32)).astype(jnp.bfloat16)
    blocks = TOKENS // TOK_DEV
    flat_routes = routes.reshape(blocks, TOK_DEV * 2)
    onehot = (flat_routes[:, :, None] == jnp.arange(EXPERTS, dtype=jnp.int32)[None, None, :]).astype(jnp.int32)
    before = jnp.cumsum(onehot, axis=1) - onehot
    slot = lax.optimization_barrier(jnp.sum(before * onehot, axis=-1)).reshape(TOKENS, 2).astype(jnp.int32)
    block_of = (jnp.arange(TOKENS, dtype=jnp.int32) // TOK_DEV)[:, None]
    dest = (routes * (blocks * CAP_DEV) + block_of * CAP_DEV + slot).astype(jnp.int32)
    buffer = jnp.zeros((EXPERTS * blocks * CAP_DEV, D), jnp.bfloat16)
    buffer = buffer.at[dest[:, 0]].set(normed).at[dest[:, 1]].set(normed)
    buffer = buffer.reshape(EXPERTS, blocks * CAP_DEV, D)
    expert_out = lax.map(expert_apply, (buffer, w_gate, w_up, w_down)).reshape(EXPERTS * blocks * CAP_DEV, D)
    first = expert_out[dest[:, 0]].astype(jnp.float32)
    second = expert_out[dest[:, 1]].astype(jnp.float32)
    mixed = state + gates[:, 0:1] * first + gates[:, 1:2] * second
    return mixed.astype(jnp.bfloat16)
```

```python
import functools

import jax
import jax.numpy as jnp
from jax import lax
from jax.experimental import pallas as pl
from jax.experimental.pallas import tpu as pltpu
from jax.sharding import PartitionSpec as P

MESH = pl.DeviceIdType.MESH
F32 = jnp.float32
BF16 = jnp.bfloat16
CHUNKS = 4


def kernel(
    n_exp, n_ten,
    ctx_hbm, proj_hbm, resid_hbm, gain_ref, routes_ref, gates_ref, wg_hbm, wu_hbm, wd_hbm,
    out_ref,
    ctx, proj, resid, wg, wu, wd,
    part, pa_out, pa_in, pb_out, pb_in,
    state, pack, rows, lhs, acc_g, acc_u, hid,
    part2, qa_out, qa_in, qb_out, qb_in, ret_out, ret_in,
    load_sem, proj_sem, gate_sem, up_sem, down_sem,
    pas, par, pbs, pbr, zs, zr, cs, cr, ys, yr, fs, fr, qas, qar, qbs, qbr, rs, rr,
):
    e = lax.axis_index("expert")
    t = lax.axis_index("tensor")
    core = lax.rem(t, 2)
    y = t // 2
    ny = n_ten // 2
    mate = y * 2 + 1 - core
    tok = state.shape[0]
    width = state.shape[1]
    cap = tok // 2
    slots = n_exp * cap
    dc = width // CHUNKS
    half = dc // 2
    total = n_ten * slots
    ff = wg.shape[1]

    def remote(src, dst, send, recv, where):
        copy = pltpu.make_async_remote_copy(
            src_ref=src, dst_ref=dst, send_sem=send, recv_sem=recv,
            device_id=where, device_id_type=MESH,
        )
        return copy

    def cols(c):
        return pl.ds(c * dc, dc)

    first_loads = [
        pltpu.make_async_copy(ctx_hbm, ctx, load_sem.at[0]),
        pltpu.make_async_copy(
            resid_hbm.at[pl.ds(pl.multiple_of(t * tok, tok), tok)], resid, load_sem.at[1]
        ),
    ]
    proj_loads = [
        pltpu.make_async_copy(proj_hbm.at[:, cols(c)], proj.at[:, cols(c)], proj_sem.at[c])
        for c in range(CHUNKS)
    ]
    gate_loads = [
        pltpu.make_async_copy(wg_hbm.at[0, cols(c)], wg.at[cols(c)], gate_sem.at[c])
        for c in range(CHUNKS)
    ]
    up_loads = [
        pltpu.make_async_copy(wu_hbm.at[0, cols(c)], wu.at[cols(c)], up_sem.at[c])
        for c in range(CHUNKS)
    ]
    down_loads = [
        pltpu.make_async_copy(wd_hbm.at[0, :, cols(c)], wd.at[:, cols(c)], down_sem.at[c])
        for c in range(CHUNKS)
    ]
    for load in first_loads + proj_loads:
        load.start()
    for c in range(CHUNKS):
        gate_loads[c].start()
        up_loads[c].start()
    for load in down_loads:
        load.start()

    others_y = [lax.rem(y + k, ny) for k in range(1, ny)]
    others_e = [lax.rem(e + k, n_exp) for k in range(1, n_exp)]

    barrier = pltpu.get_barrier_semaphore()
    pl.semaphore_signal(barrier, inc=1, device_id={"tensor": mate}, device_id_type=MESH)
    for oy in others_y:
        pl.semaphore_signal(
            barrier, inc=1, device_id={"tensor": oy * 2 + core}, device_id_type=MESH
        )
    for oe in others_e:
        pl.semaphore_signal(barrier, inc=1, device_id={"expert": oe}, device_id_type=MESH)

    own = routes_ref[pl.ds(pl.multiple_of(t * tok, tok), tok), :]
    lane = lax.broadcasted_iota(jnp.int32, (tok, 128), 1)
    lane_exp = lane // cap
    lane_slot = (lane - lane_exp * cap).astype(F32)
    m0 = jnp.where(own[:, 0:1] == lane_exp, 1.0, 0.0).astype(F32)
    m1 = jnp.where(own[:, 1:2] == lane_exp, 1.0, 0.0).astype(F32)
    ri = lax.broadcasted_iota(jnp.int32, (tok, tok), 0)
    ci = lax.broadcasted_iota(jnp.int32, (tok, tok), 1)
    lower = jnp.where(ci < ri, 1.0, 0.0).astype(BF16)
    before = jnp.dot(lower, (m0 + m1).astype(BF16), preferred_element_type=F32)
    hit = jnp.where(before == lane_slot, 1.0, 0.0)
    s0 = (m0 * hit)[:, :slots].astype(BF16)
    s1 = (m1 * hit)[:, :slots].astype(BF16)
    spread = ((m0 + m1) * hit)[:, :slots].astype(BF16)

    for load in first_loads:
        load.wait()
    pl.semaphore_wait(barrier, 1 + (ny - 1) + (n_exp - 1))

    sends = []

    def reduce_a(buf, c, out, into, send, recv):
        for oy in range(ny):
            out[c, oy] = buf[c, oy * 2 + 1 - core].astype(BF16)
        copy = remote(out.at[c], into.at[c], send.at[c], recv.at[c], {"tensor": mate})
        copy.start()
        sends.append(copy)
        return copy

    def reduce_b(buf, c, into, out, into2, send, recv):
        copies = []
        for k in range(1, ny):
            oy = others_y[k - 1]
            out[c, k - 1] = (buf[c, oy * 2 + core] + into[c, oy].astype(F32)).astype(BF16)
            copy = remote(
                out.at[c, k - 1], into2.at[c, k - 1], send.at[c, k - 1], recv.at[c, k - 1],
                {"tensor": oy * 2 + core},
            )
            copy.start()
            sends.append(copy)
            copies.append(copy)
        return copies

    def reduce_c(buf, c, into, into2):
        value = buf[c, t] + into[c, y].astype(F32)
        for k in range(1, ny):
            value = value + into2[c, k - 1].astype(F32)
        return value

    def fold(value):
        value = value.reshape(n_exp, cap, value.shape[-1])
        side = value.shape[-1] // 2
        return jnp.concatenate([value[:, :, :side], value[:, :, side:]], axis=1)

    def spans(c):
        wide = half + (128 if c == CHUNKS - 1 else 0)
        return pl.ds(c * half, wide)

    square = [jnp.zeros((tok, 1), F32)]
    pa, pb, pz, pc, py, pf = {}, {}, {}, {}, {}, {}

    def stage_a(c):
        proj_loads[c].wait()
        nt = half
        ctx_rows = ctx.shape[0]
        for n in range(dc // nt):
            sl = pl.ds(c * dc + n * nt, nt)
            value = jnp.dot(ctx[...], proj[:, sl], preferred_element_type=F32)
            part[c, :, :, n * nt:(n + 1) * nt] = value.reshape(n_ten, ctx_rows // n_ten, nt)
        pa[c] = reduce_a(part, c, pa_out, pa_in, pas, par)

    def stage_b(c):
        pa[c].wait_recv()
        pb[c] = reduce_b(part, c, pa_in, pb_out, pb_in, pbs, pbr)

    def stage_c(c):
        for copy in pb[c]:
            copy.wait_recv()
        sl = cols(c)
        value = resid[:, sl].astype(F32) + reduce_c(part, c, pa_in, pb_in)
        state[:, sl] = value
        square[0] = square[0] + jnp.sum(value * value, axis=1, keepdims=True)
        x = (value * gain_ref[:, sl].astype(F32)).astype(BF16)
        dims = (((0,), (0,)), ((), ()))
        packed = lax.dot_general(spread, x, dims, preferred_element_type=F32)
        pack[:, :, c * half:(c + 1) * half] = fold(packed).astype(BF16)
        if c == CHUNKS - 1:
            scale = lax.rsqrt(square[0] / width + 1e-05)
            scale = jnp.broadcast_to(scale, (tok, 128))
            high = scale.astype(BF16)
            low = (scale - high.astype(F32)).astype(BF16)
            both = jnp.concatenate([high, low], axis=1)
            packed = lax.dot_general(spread, both, dims, preferred_element_type=F32)
            pack[:, :, width // 2:] = fold(packed).astype(BF16)
        sp = spans(c)
        pz[c] = []
        for k in range(1, n_exp):
            oe = others_e[k - 1]
            copy = remote(
                pack.at[oe, :, sp], rows.at[t, e, :, sp], zs.at[c, k - 1], zr.at[c, k - 1],
                {"expert": oe},
            )
            copy.start()
            sends.append(copy)
            pz[c].append(copy)
        rows[t, e, :, sp] = pack[e, :, sp]

    def stage_d(c):
        for copy in pz[c]:
            copy.wait_recv()
        sp = spans(c)
        pieces = rows.at[t, :, :, sp]
        py[c] = []
        for k in range(1, ny):
            copy = remote(
                pieces, pieces, ys.at[c, k - 1], yr.at[c, k - 1],
                {"tensor": others_y[k - 1] * 2 + core},
            )
            copy.start()
            sends.append(copy)
            py[c].append(copy)
        pc[c] = remote(pieces, pieces, cs.at[c], cr.at[c], {"tensor": mate})
        pc[c].start()
        sends.append(pc[c])

    def stage_e(c):
        sp = spans(c)
        pf[c] = []
        for k in range(1, ny):
            py[c][k - 1].wait_recv()
            src = lax.rem(y - k + ny, ny) * 2 + core
            pieces = rows.at[src, :, :, sp]
            copy = remote(
                pieces, pieces, fs.at[c, k - 1], fr.at[c, k - 1], {"tensor": mate}
            )
            copy.start()
            sends.append(copy)
            pf[c].append(copy)

    mb = min(total, 128)
    nt = min(ff, 512)

    def stage_f(c):
        pc[c].wait_recv()
        for copy in pf[c]:
            copy.wait_recv()
        last = c == CHUNKS - 1
        sp = pl.ds(c * half, half)

        def unfold(i, _):
            value = rows[i, :, :, sp].astype(F32)
            at = pl.ds(pl.multiple_of(i * slots, slots), slots)
            lhs[at, c * dc:c * dc + half] = value[:, :cap].reshape(slots, half).astype(BF16)
            lhs[at, c * dc + half:(c + 1) * dc] = (
                value[:, cap:].reshape(slots, half).astype(BF16)
            )
            return 0

        lax.fori_loop(0, n_ten, unfold, 0, unroll=True)
        gate_loads[c].wait()
        up_loads[c].wait()

        def block(m, _):
            at = pl.ds(pl.multiple_of(m * mb, mb), mb)
            if last:
                per = mb // slots
                tail = rows[pl.ds(m * per, per), :, :, width // 2:].astype(F32)
                scale = (tail[:, :, :cap] + tail[:, :, cap:]).reshape(mb, 128)[:, 0:1]

            def tile(n, _):
                cs_ = pl.ds(pl.multiple_of(n * nt, nt), nt)
                left = lhs[at, cols(c)]
                g = jnp.dot(left, wg[cols(c), cs_], preferred_element_type=F32)
                u = jnp.dot(left, wu[cols(c), cs_], preferred_element_type=F32)
                if c > 0:
                    g = g + acc_g[at, cs_]
                    u = u + acc_u[at, cs_]
                if last:
                    g = g * scale
                    u = u * scale
                    hid[at, cs_] = (g / (1.0 + jnp.exp(-g)) * u).astype(BF16)
                else:
                    acc_g[at, cs_] = g
                    acc_u[at, cs_] = u
                return 0

            lax.fori_loop(0, ff // nt, tile, 0)
            return 0

        lax.fori_loop(0, total // mb, block, 0)

    order = [stage_a, stage_b, stage_c, stage_d, stage_e, stage_f]
    for s in range(CHUNKS + len(order) - 1):
        for depth, stage in enumerate(order):
            if 0 <= s - depth < CHUNKS:
                stage(s - depth)

    qa, qb, pr = {}, {}, {}

    def down_a(c):
        down_loads[c].wait()
        per = mb // slots
        wt = half

        def block(m, _):
            at = pl.ds(pl.multiple_of(m * mb, mb), mb)
            for n in range(dc // wt):
                sl = pl.ds(c * dc + n * wt, wt)
                value = jnp.dot(hid[at, :], wd[:, sl], preferred_element_type=F32)
                part2[c, pl.ds(m * per, per), :, n * wt:(n + 1) * wt] = value.reshape(
                    per, slots, wt
                )
            return 0

        lax.fori_loop(0, total // mb, block, 0)
        qa[c] = reduce_a(part2, c, qa_out, qa_in, qas, qar)

    def down_b(c):
        qa[c].wait_recv()
        qb[c] = reduce_b(part2, c, qa_in, qb_out, qb_in, qbs, qbr)

    def down_c(c):
        for copy in qb[c]:
            copy.wait_recv()
        ret_out[c] = fold(reduce_c(part2, c, qa_in, qb_in)).astype(BF16)
        pr[c] = []
        for k in range(1, n_exp):
            oe = others_e[k - 1]
            copy = remote(
                ret_out.at[c, oe], ret_in.at[c, e], rs.at[c, k - 1], rr.at[c, k - 1],
                {"expert": oe},
            )
            copy.start()
            sends.append(copy)
            pr[c].append(copy)
        ret_in[c, e] = ret_out[c, e]

    def down_d(c):
        for copy in pr[c]:
            copy.wait_recv()
        value = ret_in[c].astype(F32)
        for side in range(2):
            piece = value[:, side * cap:(side + 1) * cap].reshape(slots, half).astype(BF16)
            sl = pl.ds(c * dc + side * half, half)
            first = jnp.dot(s0, piece, preferred_element_type=F32)
            second = jnp.dot(s1, piece, preferred_element_type=F32)
            mixed = state[:, sl] + gates_ref[:, 0:1] * first + gates_ref[:, 1:2] * second
            out_ref[:, sl] = mixed.astype(BF16)

    order = [down_a, down_b, down_c, down_d]
    for s in range(CHUNKS + len(order) - 1):
        for depth, stage in enumerate(order):
            if 0 <= s - depth < CHUNKS:
                stage(s - depth)

    for copy in sends:
        copy.wait_send()


def body(context, out_proj, resid, norm_gain, routes, gates, w_gate, w_up, w_down):
    n_exp = lax.axis_size("expert")
    n_ten = lax.axis_size("tensor")
    ny = n_ten // 2
    tok = gates.shape[0]
    width = resid.shape[1]
    cap = tok // 2
    slots = n_exp * cap
    total = n_ten * slots
    ff = w_gate.shape[2]
    dc = width // CHUNKS
    half = dc // 2
    lanes = width // 2 + 128
    dma = pltpu.SemaphoreType.DMA
    hbm = pl.BlockSpec(memory_space=pl.ANY)
    vmem = pl.BlockSpec(memory_space=pltpu.VMEM)
    many = max(ny - 1, 1)
    return pl.pallas_call(
        functools.partial(kernel, n_exp, n_ten),
        out_shape=jax.ShapeDtypeStruct((tok, width), BF16),
        in_specs=[hbm, hbm, hbm, vmem, vmem, vmem, hbm, hbm, hbm],
        out_specs=vmem,
        scratch_shapes=[
            pltpu.VMEM(context.shape, BF16),
            pltpu.VMEM(out_proj.shape, BF16),
            pltpu.VMEM((tok, width), BF16),
            pltpu.VMEM((width, ff), BF16),
            pltpu.VMEM((width, ff), BF16),
            pltpu.VMEM((ff, width), BF16),
            pltpu.VMEM((CHUNKS, n_ten, tok, dc), F32),
            pltpu.VMEM((CHUNKS, ny, tok, dc), BF16),
            pltpu.VMEM((CHUNKS, ny, tok, dc), BF16),
            pltpu.VMEM((CHUNKS, many, tok, dc), BF16),
            pltpu.VMEM((CHUNKS, many, tok, dc), BF16),
            pltpu.VMEM((tok, width), F32),
            pltpu.VMEM((n_exp, 2 * cap, lanes), BF16),
            pltpu.VMEM((n_ten, n_exp, 2 * cap, lanes), BF16),
            pltpu.VMEM((total, width), BF16),
            pltpu.VMEM((total, ff), F32),
            pltpu.VMEM((total, ff), F32),
            pltpu.VMEM((total, ff), BF16),
            pltpu.VMEM((CHUNKS, n_ten, slots, dc), F32),
            pltpu.VMEM((CHUNKS, ny, slots, dc), BF16),
            pltpu.VMEM((CHUNKS, ny, slots, dc), BF16),
            pltpu.VMEM((CHUNKS, many, slots, dc), BF16),
            pltpu.VMEM((CHUNKS, many, slots, dc), BF16),
            pltpu.VMEM((CHUNKS, n_exp, 2 * cap, half), BF16),
            pltpu.VMEM((CHUNKS, n_exp, 2 * cap, half), BF16),
            dma((2,)),
            dma((CHUNKS,)),
            dma((CHUNKS,)),
            dma((CHUNKS,)),
            dma((CHUNKS,)),
            dma((CHUNKS,)),
            dma((CHUNKS,)),
            dma((CHUNKS, many)),
            dma((CHUNKS, many)),
            dma((CHUNKS, n_exp - 1)),
            dma((CHUNKS, n_exp - 1)),
            dma((CHUNKS,)),
            dma((CHUNKS,)),
            dma((CHUNKS, many)),
            dma((CHUNKS, many)),
            dma((CHUNKS, many)),
            dma((CHUNKS, many)),
            dma((CHUNKS,)),
            dma((CHUNKS,)),
            dma((CHUNKS, many)),
            dma((CHUNKS, many)),
            dma((CHUNKS, n_exp - 1)),
            dma((CHUNKS, n_exp - 1)),
        ],
        compiler_params=pltpu.CompilerParams(
            collective_id=0, has_side_effects=True, vmem_limit_bytes=62 * 1024 * 1024
        ),
    )(
        context, out_proj, resid, norm_gain.reshape(1, width), routes, gates,
        w_gate, w_up, w_down,
    )


def solution(mesh):
    in_specs = (
        P(("groups", "expert"), "tensor"),
        P("tensor", None),
        P(("groups", "expert"), None),
        P(),
        P(("groups", "expert"), None),
        P(("groups", "expert", "tensor"), None),
        P("expert", None, "tensor"),
        P("expert", None, "tensor"),
        P("expert", "tensor", None),
    )
    out_specs = P(("groups", "expert", "tensor"), None)
    return jax.shard_map(body, mesh=mesh, in_specs=in_specs, out_specs=out_specs, check_vma=False)
```

```python
import functools

import jax
import jax.numpy as jnp
from jax import lax
from jax.experimental import pallas as pl
from jax.experimental.pallas import tpu as pltpu
from jax.sharding import PartitionSpec as P

MESH = pl.DeviceIdType.MESH
F32 = jnp.float32
BF16 = jnp.bfloat16
CHUNKS = 2
BACK = 2


def kernel(
    n_exp, n_ten,
    ctx_hbm, proj_hbm, resid_hbm, gain_ref, routes_ref, gates_ref, wg_hbm, wu_hbm, wd_hbm,
    out_ref,
    ctx, proj, resid, wg, wu, wd,
    part, pa_out, pa_in, pb_out, pb_in,
    state, pack, rows, lhs, acc_g, acc_u, hid,
    part2, qa_out, qa_in, qb_out, qb_in, ret_out, ret_in,
    load_sem, proj_sem, gate_sem, up_sem, down_sem,
    pas, par, pbs, pbr, zs, zr, cs, cr, ys, yr, fs, fr, qas, qar, qbs, qbr, rs, rr,
):
    e = lax.axis_index("expert")
    t = lax.axis_index("tensor")
    core = lax.rem(t, 2)
    y = t // 2
    ny = n_ten // 2
    mate = y * 2 + 1 - core
    tok = state.shape[0]
    width = state.shape[1]
    cap = tok // 2
    slots = n_exp * cap
    dc = width // CHUNKS
    half = dc // 2
    dc2 = width // BACK
    half2 = dc2 // 2
    total = n_ten * slots
    ff = wg.shape[1]

    def remote(src, dst, send, recv, where):
        copy = pltpu.make_async_remote_copy(
            src_ref=src, dst_ref=dst, send_sem=send, recv_sem=recv,
            device_id=where, device_id_type=MESH,
        )
        return copy

    def cols(c):
        return pl.ds(c * dc, dc)

    first_loads = [
        pltpu.make_async_copy(ctx_hbm, ctx, load_sem.at[0]),
        pltpu.make_async_copy(
            resid_hbm.at[pl.ds(pl.multiple_of(t * tok, tok), tok)], resid, load_sem.at[1]
        ),
    ]
    proj_loads = [
        pltpu.make_async_copy(proj_hbm.at[:, cols(c)], proj.at[:, cols(c)], proj_sem.at[c])
        for c in range(CHUNKS)
    ]
    gate_loads = [
        pltpu.make_async_copy(wg_hbm.at[0, cols(c)], wg.at[cols(c)], gate_sem.at[c])
        for c in range(CHUNKS)
    ]
    up_loads = [
        pltpu.make_async_copy(wu_hbm.at[0, cols(c)], wu.at[cols(c)], up_sem.at[c])
        for c in range(CHUNKS)
    ]
    down_load = pltpu.make_async_copy(wd_hbm.at[0], wd, down_sem.at[0])

    others_y = [lax.rem(y + k, ny) for k in range(1, ny)]
    others_e = [lax.rem(e + k, n_exp) for k in range(1, n_exp)]

    barrier = pltpu.get_barrier_semaphore()
    pl.semaphore_signal(barrier, inc=1, device_id={"tensor": mate}, device_id_type=MESH)
    for oy in others_y:
        pl.semaphore_signal(
            barrier, inc=1, device_id={"tensor": oy * 2 + core}, device_id_type=MESH
        )
    for oe in others_e:
        pl.semaphore_signal(barrier, inc=1, device_id={"expert": oe}, device_id_type=MESH)

    for load in first_loads + proj_loads:
        load.start()

    def column(row, start):
        spot = lax.broadcasted_iota(jnp.int32, (tok, row.shape[1]), 1)
        line = lax.broadcasted_iota(jnp.int32, (tok, row.shape[1]), 0)
        return jnp.sum(jnp.where(spot == line + start, row, 0.0), axis=1, keepdims=True)

    chosen = routes_ref[...].astype(F32)
    weights = gates_ref[...]
    gate0, gate1 = column(weights[0:1], 0), column(weights[1:2], 0)
    route0 = column(chosen[0:1], t * tok).astype(jnp.int32)
    route1 = column(chosen[1:2], t * tok).astype(jnp.int32)
    lane = lax.broadcasted_iota(jnp.int32, (tok, 128), 1)
    lane_exp = lane // cap
    lane_slot = (lane - lane_exp * cap).astype(F32)
    m0 = jnp.where(route0 == lane_exp, 1.0, 0.0).astype(F32)
    m1 = jnp.where(route1 == lane_exp, 1.0, 0.0).astype(F32)
    ri = lax.broadcasted_iota(jnp.int32, (tok, tok), 0)
    ci = lax.broadcasted_iota(jnp.int32, (tok, tok), 1)
    lower = jnp.where(ci < ri, 1.0, 0.0).astype(BF16)
    before = jnp.dot(lower, (m0 + m1).astype(BF16), preferred_element_type=F32)
    hit = jnp.where(before == lane_slot, 1.0, 0.0)
    s0 = (m0 * hit)[:, :slots].astype(BF16)
    s1 = (m1 * hit)[:, :slots].astype(BF16)
    spread = ((m0 + m1) * hit)[:, :slots].astype(BF16)

    for load in first_loads:
        load.wait()
    sends = []

    def reduce_a(buf, c, out, into, send, recv):
        for oy in range(ny):
            out[c, oy] = buf[c, oy * 2 + 1 - core].astype(BF16)
        copy = remote(out.at[c], into.at[c], send.at[c], recv.at[c], {"tensor": mate})
        copy.start()
        sends.append(copy)
        return copy

    def reduce_b(buf, c, into, out, into2, send, recv):
        copies = []
        for k in range(1, ny):
            oy = others_y[k - 1]
            out[c, k - 1] = (buf[c, oy * 2 + core] + into[c, oy].astype(F32)).astype(BF16)
            copy = remote(
                out.at[c, k - 1], into2.at[c, k - 1], send.at[c, k - 1], recv.at[c, k - 1],
                {"tensor": oy * 2 + core},
            )
            copy.start()
            sends.append(copy)
            copies.append(copy)
        return copies

    def reduce_c(buf, c, into, into2):
        value = buf[c, t] + into[c, y].astype(F32)
        for k in range(1, ny):
            value = value + into2[c, k - 1].astype(F32)
        return value

    def fold(value):
        value = value.reshape(n_exp, cap, value.shape[-1])
        side = value.shape[-1] // 2
        return jnp.concatenate([value[:, :, :side], value[:, :, side:]], axis=1)

    def spans(c):
        wide = half + (128 if c == CHUNKS - 1 else 0)
        return pl.ds(c * half, wide)

    square = [jnp.zeros((tok, 1), F32)]
    pa, pb, pz, pc, py, pf = {}, {}, {}, {}, {}, {}

    def stage_a(c):
        proj_loads[c].wait()
        nt = half
        ctx_rows = ctx.shape[0]
        for n in range(dc // nt):
            sl = pl.ds(c * dc + n * nt, nt)
            value = jnp.dot(ctx[...], proj[:, sl], preferred_element_type=F32)
            part[c, :, :, n * nt:(n + 1) * nt] = value.reshape(n_ten, ctx_rows // n_ten, nt)
        if c == 0:
            pl.semaphore_wait(barrier, 1 + (ny - 1) + (n_exp - 1))
        pa[c] = reduce_a(part, c, pa_out, pa_in, pas, par)
        if c == CHUNKS - 1:
            for load in [x for pair in zip(gate_loads, up_loads) for x in pair]:
                load.start()
            down_load.start()

    def stage_b(c):
        pa[c].wait_recv()
        pb[c] = reduce_b(part, c, pa_in, pb_out, pb_in, pbs, pbr)

    def stage_c(c):
        for copy in pb[c]:
            copy.wait_recv()
        sl = cols(c)
        value = resid[:, sl].astype(F32) + reduce_c(part, c, pa_in, pb_in)
        state[:, sl] = value
        square[0] = square[0] + jnp.sum(value * value, axis=1, keepdims=True)
        x = (value * gain_ref[sl].astype(F32).reshape(1, dc)).astype(BF16)
        dims = (((0,), (0,)), ((), ()))
        packed = lax.dot_general(spread, x, dims, preferred_element_type=F32)
        pack[:, :, c * half:(c + 1) * half] = fold(packed).astype(BF16)
        if c == CHUNKS - 1:
            scale = lax.rsqrt(square[0] / width + 1e-05)
            scale = jnp.broadcast_to(scale, (tok, 128))
            high = scale.astype(BF16)
            low = (scale - high.astype(F32)).astype(BF16)
            both = jnp.concatenate([high, low], axis=1)
            packed = lax.dot_general(spread, both, dims, preferred_element_type=F32)
            pack[:, :, width // 2:] = fold(packed).astype(BF16)
        sp = spans(c)
        pz[c] = []
        for k in range(1, n_exp):
            oe = others_e[k - 1]
            copy = remote(
                pack.at[oe, :, sp], rows.at[t, e, :, sp], zs.at[c, k - 1], zr.at[c, k - 1],
                {"expert": oe},
            )
            copy.start()
            sends.append(copy)
            pz[c].append(copy)
        rows[t, e, :, sp] = pack[e, :, sp]

    hops = sorted(range(n_exp), key=lambda k: min(k, n_exp - k))

    def stage_d(c):
        sp = spans(c)
        py[c], pc[c] = {}, []
        for k in hops:
            if k > 0:
                pz[c][k - 1].wait_recv()
            src = lax.rem(e - k + n_exp, n_exp)
            piece = rows.at[t, src, :, sp]
            for q in range(1, ny):
                copy = remote(
                    piece, piece, ys.at[c, k, q - 1], yr.at[c, k, q - 1],
                    {"tensor": others_y[q - 1] * 2 + core},
                )
                copy.start()
                sends.append(copy)
                py[c][k, q] = copy
            copy = remote(piece, piece, cs.at[c, k], cr.at[c, k], {"tensor": mate})
            copy.start()
            sends.append(copy)
            pc[c].append(copy)

    def stage_e(c):
        sp = spans(c)
        pf[c] = []
        for k in hops:
            src = lax.rem(e - k + n_exp, n_exp)
            for q in range(1, ny):
                py[c][k, q].wait_recv()
                far = lax.rem(y - q + ny, ny) * 2 + core
                piece = rows.at[far, src, :, sp]
                copy = remote(
                    piece, piece, fs.at[c, k, q - 1], fr.at[c, k, q - 1], {"tensor": mate}
                )
                copy.start()
                sends.append(copy)
                pf[c].append(copy)

    mb = min(total, 128)
    nt = min(ff, 512)

    def stage_f(c):
        for copy in pc[c] + pf[c]:
            copy.wait_recv()
        last = c == CHUNKS - 1
        sp = pl.ds(c * half, half)

        def unfold(i, _):
            value = rows[i, :, :, sp].astype(F32)
            at = pl.ds(pl.multiple_of(i * slots, slots), slots)
            lhs[at, c * dc:c * dc + half] = value[:, :cap].reshape(slots, half).astype(BF16)
            lhs[at, c * dc + half:(c + 1) * dc] = (
                value[:, cap:].reshape(slots, half).astype(BF16)
            )
            return 0

        lax.fori_loop(0, n_ten, unfold, 0, unroll=True)
        gate_loads[c].wait()
        up_loads[c].wait()

        def block(m, _):
            at = pl.ds(pl.multiple_of(m * mb, mb), mb)
            if last:
                per = mb // slots
                tail = rows[pl.ds(m * per, per), :, :, width // 2:].astype(F32)
                scale = (tail[:, :, :cap] + tail[:, :, cap:]).reshape(mb, 128)[:, 0:1]

            def tile(n, _):
                cs_ = pl.ds(pl.multiple_of(n * nt, nt), nt)
                left = lhs[at, cols(c)]
                g = jnp.dot(left, wg[cols(c), cs_], preferred_element_type=F32)
                u = jnp.dot(left, wu[cols(c), cs_], preferred_element_type=F32)
                if c > 0:
                    g = g + acc_g[at, cs_]
                    u = u + acc_u[at, cs_]
                if last:
                    g = g * scale
                    u = u * scale
                    hid[at, cs_] = (g / (1.0 + jnp.exp(-g)) * u).astype(BF16)
                else:
                    acc_g[at, cs_] = g
                    acc_u[at, cs_] = u
                return 0

            lax.fori_loop(0, ff // nt, tile, 0)
            return 0

        lax.fori_loop(0, total // mb, block, 0)

    order = [stage_a, stage_b, stage_c, stage_d, stage_e, stage_f]
    for s in range(CHUNKS + len(order) - 1):
        for depth, stage in enumerate(order):
            if 0 <= s - depth < CHUNKS:
                stage(s - depth)

    qa, qb, pr = {}, {}, {}

    def down_a(c):
        if c == 0:
            down_load.wait()
        per = mb // slots
        wt = half2

        def block(m, _):
            at = pl.ds(pl.multiple_of(m * mb, mb), mb)
            for n in range(dc2 // wt):
                sl = pl.ds(c * dc2 + n * wt, wt)
                value = jnp.dot(hid[at, :], wd[:, sl], preferred_element_type=F32)
                part2[c, pl.ds(m * per, per), :, n * wt:(n + 1) * wt] = value.reshape(
                    per, slots, wt
                )
            return 0

        lax.fori_loop(0, total // mb, block, 0)
        qa[c] = reduce_a(part2, c, qa_out, qa_in, qas, qar)

    def down_b(c):
        qa[c].wait_recv()
        qb[c] = reduce_b(part2, c, qa_in, qb_out, qb_in, qbs, qbr)

    def down_c(c):
        for copy in qb[c]:
            copy.wait_recv()
        ret_out[c] = fold(reduce_c(part2, c, qa_in, qb_in)).astype(BF16)
        pr[c] = []
        for k in range(1, n_exp):
            oe = others_e[k - 1]
            copy = remote(
                ret_out.at[c, oe], ret_in.at[c, e], rs.at[c, k - 1], rr.at[c, k - 1],
                {"expert": oe},
            )
            copy.start()
            sends.append(copy)
            pr[c].append(copy)
        ret_in[c, e] = ret_out[c, e]

    def down_d(c):
        for copy in pr[c]:
            copy.wait_recv()
        value = ret_in[c].astype(F32)
        for side in range(2):
            piece = value[:, side * cap:(side + 1) * cap].reshape(slots, half2).astype(BF16)
            sl = pl.ds(c * dc2 + side * half2, half2)
            first = jnp.dot(s0, piece, preferred_element_type=F32)
            second = jnp.dot(s1, piece, preferred_element_type=F32)
            mixed = state[:, sl] + gate0 * first + gate1 * second
            out_ref[:, sl] = mixed.astype(BF16)

    order = [down_a, down_b, down_c, down_d]
    for s in range(BACK + len(order) - 1):
        for depth, stage in enumerate(order):
            if 0 <= s - depth < BACK:
                stage(s - depth)

    for copy in sends:
        copy.wait_send()


def body(context, out_proj, resid, norm_gain, routes, gates, w_gate, w_up, w_down):
    n_exp = lax.axis_size("expert")
    n_ten = lax.axis_size("tensor")
    ny = n_ten // 2
    tok = gates.shape[0]
    width = resid.shape[1]
    cap = tok // 2
    slots = n_exp * cap
    total = n_ten * slots
    ff = w_gate.shape[2]
    dc = width // CHUNKS
    dc2 = width // BACK
    half2 = dc2 // 2
    lanes = width // 2 + 128
    dma = pltpu.SemaphoreType.DMA
    hbm = pl.BlockSpec(memory_space=pl.ANY)
    vmem = pl.BlockSpec(memory_space=pltpu.VMEM)
    many = max(ny - 1, 1)
    return pl.pallas_call(
        functools.partial(kernel, n_exp, n_ten),
        out_shape=jax.ShapeDtypeStruct((tok, width), BF16),
        in_specs=[hbm, hbm, hbm, vmem, vmem, vmem, hbm, hbm, hbm],
        out_specs=vmem,
        scratch_shapes=[
            pltpu.VMEM(context.shape, BF16),
            pltpu.VMEM(out_proj.shape, BF16),
            pltpu.VMEM((tok, width), BF16),
            pltpu.VMEM((width, ff), BF16),
            pltpu.VMEM((width, ff), BF16),
            pltpu.VMEM((ff, width), BF16),
            pltpu.VMEM((CHUNKS, n_ten, tok, dc), F32),
            pltpu.VMEM((CHUNKS, ny, tok, dc), BF16),
            pltpu.VMEM((CHUNKS, ny, tok, dc), BF16),
            pltpu.VMEM((CHUNKS, many, tok, dc), BF16),
            pltpu.VMEM((CHUNKS, many, tok, dc), BF16),
            pltpu.VMEM((tok, width), F32),
            pltpu.VMEM((n_exp, 2 * cap, lanes), BF16),
            pltpu.VMEM((n_ten, n_exp, 2 * cap, lanes), BF16),
            pltpu.VMEM((total, width), BF16),
            pltpu.VMEM((total, ff), F32),
            pltpu.VMEM((total, ff), F32),
            pltpu.VMEM((total, ff), BF16),
            pltpu.VMEM((BACK, n_ten, slots, dc2), F32),
            pltpu.VMEM((BACK, ny, slots, dc2), BF16),
            pltpu.VMEM((BACK, ny, slots, dc2), BF16),
            pltpu.VMEM((BACK, many, slots, dc2), BF16),
            pltpu.VMEM((BACK, many, slots, dc2), BF16),
            pltpu.VMEM((BACK, n_exp, 2 * cap, half2), BF16),
            pltpu.VMEM((BACK, n_exp, 2 * cap, half2), BF16),
            dma((2,)),
            dma((CHUNKS,)),
            dma((CHUNKS,)),
            dma((CHUNKS,)),
            dma((CHUNKS,)),
            dma((CHUNKS,)),
            dma((CHUNKS,)),
            dma((CHUNKS, many)),
            dma((CHUNKS, many)),
            dma((CHUNKS, n_exp - 1)),
            dma((CHUNKS, n_exp - 1)),
            dma((CHUNKS, n_exp)),
            dma((CHUNKS, n_exp)),
            dma((CHUNKS, n_exp, many)),
            dma((CHUNKS, n_exp, many)),
            dma((CHUNKS, n_exp, many)),
            dma((CHUNKS, n_exp, many)),
            dma((BACK,)),
            dma((BACK,)),
            dma((BACK, many)),
            dma((BACK, many)),
            dma((BACK, n_exp - 1)),
            dma((BACK, n_exp - 1)),
        ],
        compiler_params=pltpu.CompilerParams(
            collective_id=0, has_side_effects=True, vmem_limit_bytes=62 * 1024 * 1024
        ),
    )(
        context, out_proj, resid, norm_gain, routes.T, gates.T,
        w_gate, w_up, w_down,
    )


def solution(mesh):
    in_specs = (
        P(("groups", "expert"), "tensor"),
        P("tensor", None),
        P(("groups", "expert"), None),
        P(),
        P(("groups", "expert"), None),
        P(("groups", "expert", "tensor"), None),
        P("expert", None, "tensor"),
        P("expert", None, "tensor"),
        P("expert", "tensor", None),
    )
    out_specs = P(("groups", "expert", "tensor"), None)
    return jax.shard_map(body, mesh=mesh, in_specs=in_specs, out_specs=out_specs, check_vma=False)
```

```python
import functools

import jax
import jax.numpy as jnp
from jax import lax
from jax.experimental import pallas as pl
from jax.experimental.pallas import tpu as pltpu
from jax.sharding import PartitionSpec as P

MESH = pl.DeviceIdType.MESH
F32 = jnp.float32
BF16 = jnp.bfloat16
CHUNKS = 2
BACK = 2


def kernel(
    n_exp, n_ten,
    ctx_hbm, proj_hbm, resid_hbm, gain_ref, routes_ref, gates_ref, wg_hbm, wu_hbm, wd_hbm,
    out_ref,
    ctx, proj, resid, wg, wu, wd,
    part, pa_out, pa_in, pb_out, pb_in,
    state, pack, rows, lhs, acc_g, acc_u, hid,
    part2, qa_out, qa_in, qb_out, qb_in, ret_out, ret_in,
    load_sem, proj_sem, gate_sem, up_sem, down_sem,
    pas, par, pbs, pbr, zs, zr, cs, cr, ys, yr, fs, fr, qas, qar, qbs, qbr, rs, rr,
):
    e = lax.axis_index("expert")
    t = lax.axis_index("tensor")
    core = lax.rem(t, 2)
    y = t // 2
    ny = n_ten // 2
    mate = y * 2 + 1 - core
    tok = state.shape[0]
    width = state.shape[1]
    cap = tok // 2
    slots = n_exp * cap
    dc = width // CHUNKS
    half = dc // 2
    dc2 = width // BACK
    half2 = dc2 // 2
    total = n_ten * slots
    ff = wg.shape[1]

    def remote(src, dst, send, recv, where):
        copy = pltpu.make_async_remote_copy(
            src_ref=src, dst_ref=dst, send_sem=send, recv_sem=recv,
            device_id=where, device_id_type=MESH,
        )
        return copy

    def cols(c):
        return pl.ds(c * dc, dc)

    first_loads = [
        pltpu.make_async_copy(ctx_hbm, ctx, load_sem.at[0]),
        pltpu.make_async_copy(
            resid_hbm.at[pl.ds(pl.multiple_of(t * tok, tok), tok)], resid, load_sem.at[1]
        ),
    ]
    proj_loads = [
        pltpu.make_async_copy(proj_hbm.at[:, cols(c)], proj.at[:, cols(c)], proj_sem.at[c])
        for c in range(CHUNKS)
    ]
    gate_loads = [
        pltpu.make_async_copy(wg_hbm.at[0, cols(c)], wg.at[cols(c)], gate_sem.at[c])
        for c in range(CHUNKS)
    ]
    up_loads = [
        pltpu.make_async_copy(wu_hbm.at[0, cols(c)], wu.at[cols(c)], up_sem.at[c])
        for c in range(CHUNKS)
    ]
    down_load = pltpu.make_async_copy(wd_hbm.at[0], wd, down_sem.at[0])

    others_y = [lax.rem(y + k, ny) for k in range(1, ny)]
    others_e = [lax.rem(e + k, n_exp) for k in range(1, n_exp)]

    barrier = pltpu.get_barrier_semaphore()
    pl.semaphore_signal(barrier, inc=1, device_id={"tensor": mate}, device_id_type=MESH)
    for oy in others_y:
        pl.semaphore_signal(
            barrier, inc=1, device_id={"tensor": oy * 2 + core}, device_id_type=MESH
        )
    for oe in others_e:
        pl.semaphore_signal(barrier, inc=1, device_id={"expert": oe}, device_id_type=MESH)

    for load in first_loads + proj_loads:
        load.start()

    def column(row, start):
        spot = lax.broadcasted_iota(jnp.int32, (tok, row.shape[1]), 1)
        line = lax.broadcasted_iota(jnp.int32, (tok, row.shape[1]), 0)
        return jnp.sum(jnp.where(spot == line + start, row, 0.0), axis=1, keepdims=True)

    chosen = routes_ref[...].astype(F32)
    weights = gates_ref[...]
    gate0, gate1 = column(weights[0:1], 0), column(weights[1:2], 0)
    route0 = column(chosen[0:1], t * tok).astype(jnp.int32)
    route1 = column(chosen[1:2], t * tok).astype(jnp.int32)
    lane = lax.broadcasted_iota(jnp.int32, (tok, 128), 1)
    lane_exp = lane // cap
    lane_slot = (lane - lane_exp * cap).astype(F32)
    m0 = jnp.where(route0 == lane_exp, 1.0, 0.0).astype(F32)
    m1 = jnp.where(route1 == lane_exp, 1.0, 0.0).astype(F32)
    ri = lax.broadcasted_iota(jnp.int32, (tok, tok), 0)
    ci = lax.broadcasted_iota(jnp.int32, (tok, tok), 1)
    lower = jnp.where(ci < ri, 1.0, 0.0).astype(BF16)
    before = jnp.dot(lower, (m0 + m1).astype(BF16), preferred_element_type=F32)
    hit = jnp.where(before == lane_slot, 1.0, 0.0)
    s0 = (m0 * hit)[:, :slots].astype(BF16)
    s1 = (m1 * hit)[:, :slots].astype(BF16)
    spread = ((m0 + m1) * hit)[:, :slots].astype(BF16)

    for load in first_loads:
        load.wait()
    sends = []

    def reduce_a(buf, c, out, into, send, recv):
        for oy in range(ny):
            out[c, oy] = buf[c, oy * 2 + 1 - core].astype(BF16)
        copy = remote(out.at[c], into.at[c], send.at[c], recv.at[c], {"tensor": mate})
        copy.start()
        sends.append(copy)
        return copy

    def reduce_b(buf, c, into, out, into2, send, recv):
        copies = []
        for k in range(1, ny):
            oy = others_y[k - 1]
            out[c, k - 1] = (buf[c, oy * 2 + core] + into[c, oy].astype(F32)).astype(BF16)
            copy = remote(
                out.at[c, k - 1], into2.at[c, k - 1], send.at[c, k - 1], recv.at[c, k - 1],
                {"tensor": oy * 2 + core},
            )
            copy.start()
            sends.append(copy)
            copies.append(copy)
        return copies

    def reduce_c(buf, c, into, into2):
        value = buf[c, t] + into[c, y].astype(F32)
        for k in range(1, ny):
            value = value + into2[c, k - 1].astype(F32)
        return value

    def fold(value):
        value = value.reshape(n_exp, cap, value.shape[-1])
        side = value.shape[-1] // 2
        return jnp.concatenate([value[:, :, :side], value[:, :, side:]], axis=1)

    def spans(c):
        wide = half + (128 if c == CHUNKS - 1 else 0)
        return pl.ds(c * half, wide)

    square = [jnp.zeros((tok, 1), F32)]
    pa, pb, pz, pc, py, pf = {}, {}, {}, {}, {}, {}

    def stage_a(c):
        proj_loads[c].wait()
        nt = half
        ctx_rows = ctx.shape[0]
        for n in range(dc // nt):
            sl = pl.ds(c * dc + n * nt, nt)
            value = jnp.dot(ctx[...], proj[:, sl], preferred_element_type=F32)
            part[c, :, :, n * nt:(n + 1) * nt] = value.reshape(n_ten, ctx_rows // n_ten, nt)
        if c == 0:
            pl.semaphore_wait(barrier, 1 + (ny - 1) + (n_exp - 1))
        pa[c] = reduce_a(part, c, pa_out, pa_in, pas, par)
        if c == 0:
            for load in [x for pair in zip(gate_loads, up_loads) for x in pair]:
                load.start()
            down_load.start()

    def stage_b(c):
        pa[c].wait_recv()
        pb[c] = reduce_b(part, c, pa_in, pb_out, pb_in, pbs, pbr)

    def stage_c(c):
        for copy in pb[c]:
            copy.wait_recv()
        sl = cols(c)
        value = resid[:, sl].astype(F32) + reduce_c(part, c, pa_in, pb_in)
        state[:, sl] = value
        square[0] = square[0] + jnp.sum(value * value, axis=1, keepdims=True)
        x = (value * gain_ref[sl].astype(F32).reshape(1, dc)).astype(BF16)
        dims = (((0,), (0,)), ((), ()))
        packed = lax.dot_general(spread, x, dims, preferred_element_type=F32)
        pack[:, :, c * half:(c + 1) * half] = fold(packed).astype(BF16)
        if c == CHUNKS - 1:
            scale = lax.rsqrt(square[0] / width + 1e-05)
            scale = jnp.broadcast_to(scale, (tok, 128))
            high = scale.astype(BF16)
            low = (scale - high.astype(F32)).astype(BF16)
            both = jnp.concatenate([high, low], axis=1)
            packed = lax.dot_general(spread, both, dims, preferred_element_type=F32)
            pack[:, :, width // 2:] = fold(packed).astype(BF16)
        sp = spans(c)
        pz[c] = []
        for k in range(1, n_exp):
            oe = others_e[k - 1]
            copy = remote(
                pack.at[oe, :, sp], rows.at[t, e, :, sp], zs.at[c, k - 1], zr.at[c, k - 1],
                {"expert": oe},
            )
            copy.start()
            sends.append(copy)
            pz[c].append(copy)
        rows[t, e, :, sp] = pack[e, :, sp]

    hops = sorted(range(n_exp), key=lambda k: min(k, n_exp - k))

    def stage_d(c):
        sp = spans(c)
        py[c], pc[c] = {}, []
        for k in hops:
            if k > 0:
                pz[c][k - 1].wait_recv()
            src = lax.rem(e - k + n_exp, n_exp)
            piece = rows.at[t, src, :, sp]
            for q in range(1, ny):
                copy = remote(
                    piece, piece, ys.at[c, k, q - 1], yr.at[c, k, q - 1],
                    {"tensor": others_y[q - 1] * 2 + core},
                )
                copy.start()
                sends.append(copy)
                py[c][k, q] = copy
            copy = remote(piece, piece, cs.at[c, k], cr.at[c, k], {"tensor": mate})
            copy.start()
            sends.append(copy)
            pc[c].append(copy)

    def stage_e(c):
        sp = spans(c)
        pf[c] = []
        for k in hops:
            src = lax.rem(e - k + n_exp, n_exp)
            for q in range(1, ny):
                py[c][k, q].wait_recv()
                far = lax.rem(y - q + ny, ny) * 2 + core
                piece = rows.at[far, src, :, sp]
                copy = remote(
                    piece, piece, fs.at[c, k, q - 1], fr.at[c, k, q - 1], {"tensor": mate}
                )
                copy.start()
                sends.append(copy)
                pf[c].append(copy)

    mb = min(total, 128)
    nt = min(ff, 512)

    def stage_f(c):
        for copy in pc[c] + pf[c]:
            copy.wait_recv()
        last = c == CHUNKS - 1
        sp = pl.ds(c * half, half)

        def unfold(i, _):
            value = rows[i, :, :, sp].astype(F32)
            at = pl.ds(pl.multiple_of(i * slots, slots), slots)
            lhs[at, c * dc:c * dc + half] = value[:, :cap].reshape(slots, half).astype(BF16)
            lhs[at, c * dc + half:(c + 1) * dc] = (
                value[:, cap:].reshape(slots, half).astype(BF16)
            )
            return 0

        lax.fori_loop(0, n_ten, unfold, 0, unroll=True)
        gate_loads[c].wait()
        up_loads[c].wait()

        def block(m, _):
            at = pl.ds(pl.multiple_of(m * mb, mb), mb)
            if last:
                per = mb // slots
                tail = rows[pl.ds(m * per, per), :, :, width // 2:].astype(F32)
                scale = (tail[:, :, :cap] + tail[:, :, cap:]).reshape(mb, 128)[:, 0:1]

            def tile(n, _):
                cs_ = pl.ds(pl.multiple_of(n * nt, nt), nt)
                left = lhs[at, cols(c)]
                g = jnp.dot(left, wg[cols(c), cs_], preferred_element_type=F32)
                u = jnp.dot(left, wu[cols(c), cs_], preferred_element_type=F32)
                if c > 0:
                    g = g + acc_g[at, cs_]
                    u = u + acc_u[at, cs_]
                if last:
                    g = g * scale
                    u = u * scale
                    hid[at, cs_] = (g / (1.0 + jnp.exp(-g)) * u).astype(BF16)
                else:
                    acc_g[at, cs_] = g
                    acc_u[at, cs_] = u
                return 0

            lax.fori_loop(0, ff // nt, tile, 0, unroll=True)
            return 0

        lax.fori_loop(0, total // mb, block, 0)

    order = [stage_a, stage_b, stage_c, stage_d, stage_e, stage_f]
    for s in range(CHUNKS + len(order) - 1):
        for depth, stage in enumerate(order):
            if 0 <= s - depth < CHUNKS:
                stage(s - depth)

    qa, qb, pr = {}, {}, {}

    def down_a(c):
        if c == 0:
            down_load.wait()
        per = mb // slots
        wt = half2

        def block(m, _):
            at = pl.ds(pl.multiple_of(m * mb, mb), mb)
            for n in range(dc2 // wt):
                sl = pl.ds(c * dc2 + n * wt, wt)
                value = jnp.dot(hid[at, :], wd[:, sl], preferred_element_type=F32)
                part2[c, pl.ds(m * per, per), :, n * wt:(n + 1) * wt] = value.reshape(
                    per, slots, wt
                )
            return 0

        lax.fori_loop(0, total // mb, block, 0)
        qa[c] = reduce_a(part2, c, qa_out, qa_in, qas, qar)

    def down_b(c):
        qa[c].wait_recv()
        qb[c] = reduce_b(part2, c, qa_in, qb_out, qb_in, qbs, qbr)

    def down_c(c):
        for copy in qb[c]:
            copy.wait_recv()
        ret_out[c] = fold(reduce_c(part2, c, qa_in, qb_in)).astype(BF16)
        pr[c] = []
        for k in range(1, n_exp):
            oe = others_e[k - 1]
            copy = remote(
                ret_out.at[c, oe], ret_in.at[c, e], rs.at[c, k - 1], rr.at[c, k - 1],
                {"expert": oe},
            )
            copy.start()
            sends.append(copy)
            pr[c].append(copy)
        ret_in[c, e] = ret_out[c, e]

    def down_d(c):
        for copy in pr[c]:
            copy.wait_recv()
        value = ret_in[c].astype(F32)
        for side in range(2):
            piece = value[:, side * cap:(side + 1) * cap].reshape(slots, half2).astype(BF16)
            sl = pl.ds(c * dc2 + side * half2, half2)
            first = jnp.dot(s0, piece, preferred_element_type=F32)
            second = jnp.dot(s1, piece, preferred_element_type=F32)
            mixed = state[:, sl] + gate0 * first + gate1 * second
            out_ref[:, sl] = mixed.astype(BF16)

    order = [down_a, down_b, down_c, down_d]
    for s in range(BACK + len(order) - 1):
        for depth, stage in enumerate(order):
            if 0 <= s - depth < BACK:
                stage(s - depth)

    for copy in sends:
        copy.wait_send()


def body(context, out_proj, resid, norm_gain, routes, gates, w_gate, w_up, w_down):
    n_exp = lax.axis_size("expert")
    n_ten = lax.axis_size("tensor")
    ny = n_ten // 2
    tok = gates.shape[0]
    width = resid.shape[1]
    cap = tok // 2
    slots = n_exp * cap
    total = n_ten * slots
    ff = w_gate.shape[2]
    dc = width // CHUNKS
    dc2 = width // BACK
    half2 = dc2 // 2
    lanes = width // 2 + 128
    dma = pltpu.SemaphoreType.DMA
    hbm = pl.BlockSpec(memory_space=pl.ANY)
    vmem = pl.BlockSpec(memory_space=pltpu.VMEM)
    many = max(ny - 1, 1)
    return pl.pallas_call(
        functools.partial(kernel, n_exp, n_ten),
        out_shape=jax.ShapeDtypeStruct((tok, width), BF16),
        in_specs=[hbm, hbm, hbm, vmem, vmem, vmem, hbm, hbm, hbm],
        out_specs=vmem,
        scratch_shapes=[
            pltpu.VMEM(context.shape, BF16),
            pltpu.VMEM(out_proj.shape, BF16),
            pltpu.VMEM((tok, width), BF16),
            pltpu.VMEM((width, ff), BF16),
            pltpu.VMEM((width, ff), BF16),
            pltpu.VMEM((ff, width), BF16),
            pltpu.VMEM((CHUNKS, n_ten, tok, dc), F32),
            pltpu.VMEM((CHUNKS, ny, tok, dc), BF16),
            pltpu.VMEM((CHUNKS, ny, tok, dc), BF16),
            pltpu.VMEM((CHUNKS, many, tok, dc), BF16),
            pltpu.VMEM((CHUNKS, many, tok, dc), BF16),
            pltpu.VMEM((tok, width), F32),
            pltpu.VMEM((n_exp, 2 * cap, lanes), BF16),
            pltpu.VMEM((n_ten, n_exp, 2 * cap, lanes), BF16),
            pltpu.VMEM((total, width), BF16),
            pltpu.VMEM((total, ff), F32),
            pltpu.VMEM((total, ff), F32),
            pltpu.VMEM((total, ff), BF16),
            pltpu.VMEM((BACK, n_ten, slots, dc2), F32),
            pltpu.VMEM((BACK, ny, slots, dc2), BF16),
            pltpu.VMEM((BACK, ny, slots, dc2), BF16),
            pltpu.VMEM((BACK, many, slots, dc2), BF16),
            pltpu.VMEM((BACK, many, slots, dc2), BF16),
            pltpu.VMEM((BACK, n_exp, 2 * cap, half2), BF16),
            pltpu.VMEM((BACK, n_exp, 2 * cap, half2), BF16),
            dma((2,)),
            dma((CHUNKS,)),
            dma((CHUNKS,)),
            dma((CHUNKS,)),
            dma((CHUNKS,)),
            dma((CHUNKS,)),
            dma((CHUNKS,)),
            dma((CHUNKS, many)),
            dma((CHUNKS, many)),
            dma((CHUNKS, n_exp - 1)),
            dma((CHUNKS, n_exp - 1)),
            dma((CHUNKS, n_exp)),
            dma((CHUNKS, n_exp)),
            dma((CHUNKS, n_exp, many)),
            dma((CHUNKS, n_exp, many)),
            dma((CHUNKS, n_exp, many)),
            dma((CHUNKS, n_exp, many)),
            dma((BACK,)),
            dma((BACK,)),
            dma((BACK, many)),
            dma((BACK, many)),
            dma((BACK, n_exp - 1)),
            dma((BACK, n_exp - 1)),
        ],
        compiler_params=pltpu.CompilerParams(
            collective_id=0, has_side_effects=True, vmem_limit_bytes=62 * 1024 * 1024
        ),
    )(
        context, out_proj, resid, norm_gain, routes.T, gates.T,
        w_gate, w_up, w_down,
    )


def solution(mesh):
    in_specs = (
        P(("groups", "expert"), "tensor"),
        P("tensor", None),
        P(("groups", "expert"), None),
        P(),
        P(("groups", "expert"), None),
        P(("groups", "expert", "tensor"), None),
        P("expert", None, "tensor"),
        P("expert", None, "tensor"),
        P("expert", "tensor", None),
    )
    out_specs = P(("groups", "expert", "tensor"), None)
    return jax.shard_map(body, mesh=mesh, in_specs=in_specs, out_specs=out_specs, check_vma=False)
```
